1024 devices in a mesh: row: 8 (over y_lo, core), col: 128 (over x, y_hi, z).
Axes of the slice: x: 4, y: 8 (y_hi: 2, y_lo: 4; y = y_hi * 4 + y_lo), z: 16, core: 2. Of those that a mesh axis runs over, the one named last changes fastest.
Arguments:
- tiles: float32 [8, 128, 16, 128, 128], P('row', 'col'), may hold values from 0 to 0.01953125
- coords: int32 [8, 128, 2, 16], P('row', 'col'), may hold values from 0 to 31, as said below
- counts: int32 [8, 128], P('row', 'col'), may hold values from 2 to 16
- basis: float32 [32, 524288], P(None, 'col'), may hold values from -6 to 6
Outputs:
- image: float32 [32, 16384], P(None, ('row', 'col'))
- back_image: float32 [32, 524288], P(None, 'col')
The draws below stay inside these ranges and needn't reach their ends.
Inputs may be any that keep to these rules, and one draw needn't show every extreme that they name: `coords`: within one device the 16 positions are distinct; index 0 is below 16, index 1 below 32.
All inputs are finite; a program needn't handle non-finite values.
Results may differ from the reference program's by a relative error of at most 0.0003.
Values sent between devices are 32-bit elements; how exact they have to be, the bound alone decides.
No kernel may reach another device: no remote copies, remote signals or barrier semaphores. Data moves between devices by JAX's collectives and lax.ppermute only.
A program may use at most 32 MiB of HBM per device.

```python
import jax
import jax.numpy as jnp
from jax import lax

K = 32
TILE = 128
RT = 16
CT = 32
TILES_DEV = 16
M = 16384
N = 524288
N_ROW = 8
N_COL = 128


def draw_coords(key, part):
    key = jax.random.fold_in(key, 11)
    devices = N_ROW * N_COL
    places = RT * CT
    key_perm, key_pick, key_mid = jax.random.split(key, 3)
    keys = jax.random.split(key_perm, devices)
    orders = jax.vmap(lambda one_key: jax.random.permutation(one_key, places)[:TILES_DEV])(keys).astype(jnp.int32)
    middle = (jax.random.permutation(key_mid, places - 2)[:TILES_DEV - 2] + 1).astype(jnp.int32)
    special = jnp.concatenate([jnp.array([places - 1, 0], jnp.int32), middle])
    pick = jax.random.randint(key_pick, (), 0, devices)
    chosen = (jnp.arange(devices) == pick)[:, None]
    orders = jnp.where(chosen, special[None, :], orders)
    stacked = jnp.stack([orders // CT, orders % CT], axis=1)
    return stacked.reshape(N_ROW, N_COL, 2, TILES_DEV).astype(jnp.int32)


def draw_counts(key, part):
    key = jax.random.fold_in(key, 12)
    devices = N_ROW * N_COL
    key_shift, key_pick = jax.random.split(key)
    shifts = jax.random.randint(key_shift, (devices,), 0, 4)
    values = TILES_DEV // jnp.left_shift(jnp.ones_like(shifts), shifts)
    pick = jax.random.randint(key_pick, (), 0, devices)
    index = jnp.arange(devices)
    values = jnp.where(index == pick, TILES_DEV, jnp.where(index == (pick + 1) % devices, TILES_DEV // 8, values))
    return values.reshape(N_ROW, N_COL).astype(jnp.int32)


def block_levels(rng, shape, cuts, least, high):
    factor_of = 1.0
    for dim, parts in cuts:
        draws = jax.random.uniform(jax.random.fold_in(jax.random.fold_in(rng, 6), dim), (parts,), jnp.float32, least / len(cuts), high / len(cuts))
        factor_of = factor_of * jnp.repeat(jnp.exp(draws), shape[dim] // parts).reshape((-1,) + (1,) * (len(shape) - 1 - dim))
    return factor_of


def bell_draw(key, dims, deviation, limit, cuts=(), held_as=jnp.bfloat16):
    level = block_levels(key, dims, cuts, -0.22, 0.18) if cuts else 1.0
    entries = jax.random.normal(key, dims, jnp.float32) * deviation * level
    return jnp.minimum(jnp.maximum(entries, -limit), limit).astype(held_as)


def setup_inputs(seed: int = 0) -> dict:
    seeds = jax.random.split(jax.random.key(seed), 5)
    tiles = jnp.clip(0.01953125 * jax.random.uniform(seeds[0], (N_ROW, N_COL, TILES_DEV, TILE, TILE), jnp.float32) ** block_levels(seeds[0], (N_ROW, N_COL, TILES_DEV, TILE, TILE), ((0, 8), (1, 128)), -0.2, 0.2), 0.0, 0.01953125)
    coords = draw_coords(jax.random.fold_in(seeds[4], 71), 0)
    counts = draw_counts(jax.random.fold_in(seeds[4], 71), 0)
    basis = bell_draw(seeds[3], (K, N), 1.0, 6.0, ((1, 128),), jnp.float32)
    return {"tiles": tiles, "coords": coords, "counts": counts, "basis": basis}


def reference(tiles, coords, counts, basis):
    devices = N_ROW * N_COL
    flat_tiles = tiles.reshape(devices, TILES_DEV, TILE, TILE)
    flat_coords = coords.reshape(devices, 2, TILES_DEV)
    flat_counts = counts.reshape(devices)
    device_ids = jnp.arange(devices, dtype=jnp.int32)
    dev_rows = device_ids // N_COL
    dev_cols = device_ids % N_COL
    slot_ids = jnp.arange(TILES_DEV, dtype=jnp.int32)
    basis_tiles = basis.reshape(K, CT * N_COL, TILE)

    def forward(running, item):
        tile_set, place, live_count, dev_row, dev_col = item
        live_mask = (slot_ids < live_count).astype(jnp.float32)
        grow = dev_row * RT + place[0]
        gcol = dev_col * CT + place[1]
        gathered = basis_tiles[:, gcol, :]
        product = jnp.einsum("sij,ksj->ksi", tile_set, gathered, precision=lax.Precision.HIGHEST)
        product = product * live_mask[None, :, None]
        return running.at[:, grow, :].add(product), None

    start = jnp.zeros((K, RT * N_ROW, TILE), jnp.float32)
    items = (flat_tiles, flat_coords, flat_counts, dev_rows, dev_cols)
    image_tiles, _ = lax.scan(forward, start, items)
    image = image_tiles.reshape(K, M)

    def backward(running, item):
        tile_set, place, live_count, dev_row, dev_col = item
        live_mask = (slot_ids < live_count).astype(jnp.float32)
        grow = dev_row * RT + place[0]
        gcol = dev_col * CT + place[1]
        gathered = image_tiles[:, grow, :]
        product = jnp.einsum("sij,ksi->ksj", tile_set, gathered, precision=lax.Precision.HIGHEST)
        product = product * live_mask[None, :, None]
        return running.at[:, gcol, :].add(product), None

    start_back = jnp.zeros((K, CT * N_COL, TILE), jnp.float32)
    back_tiles, _ = lax.scan(backward, start_back, items)
    return image, back_tiles.reshape(K, N)
```

```python
import jax
import jax.numpy as jnp
from jax import lax
from jax.experimental import pallas as pl
from jax.experimental.pallas import tpu as pltpu
from jax.sharding import Mesh
from jax.sharding import PartitionSpec as P

K = 32
TILE = 128
RT = 16
CT = 32
SLOTS = 16

AXES = ("yl", "core", "x", "yh", "zh", "zl")
SIZES = (4, 2, 4, 2, 4, 4)
NEAR = ("x", "zl")
FAR = ("yh", "zh")


def split(value):
    high = value.astype(jnp.bfloat16)
    low = (value - high.astype(jnp.float32)).astype(jnp.bfloat16)
    return high, low


def dot3(left, right, contract):
    lh, ll = left
    rh, rl = right
    dims = (((1,), (contract,)), ((), ()))

    def dot(a, b):
        return lax.dot_general(a, b, dims, preferred_element_type=jnp.float32)

    return dot(lh, rh) + (dot(ll, rh) + dot(lh, rl))


def forward_kernel(coords, counts, tiles, basis, part):
    part[...] = jnp.zeros_like(part)
    for s in range(SLOTS):

        @pl.when(s < counts[0])
        def _():
            row = coords[0, s]
            col = pl.multiple_of(coords[1, s] * TILE, TILE)
            part[row] += dot3(split(basis[:, pl.ds(col, TILE)]), split(tiles[s]), 1)


def backward_kernel(coords, counts, core, tiles, image, keep, send, acc):
    acc[...] = jnp.zeros_like(acc)
    for s in range(SLOTS):

        @pl.when(s < counts[0])
        def _():
            row = coords[0, s]
            col = coords[1, s]
            acc[col] += dot3(split(image[row]), split(tiles[s]), 0)

    half = CT // 2
    mine = core[0] * half
    keep[...] = acc[pl.ds(mine, half)]
    send[...] = acc[pl.ds(half - mine, half)]


def sum_copies_kernel(parts, copies):
    total = parts[0]
    for p in range(1, parts.shape[0]):
        total = total + parts[p]
    for p in range(copies.shape[0]):
        copies[p] = total


def join_kernel(core, mine, other, back):
    half = CT // 2
    for j in range(half):
        own = pl.multiple_of((core[0] * half + j) * TILE, TILE)
        far = pl.multiple_of(((1 - core[0]) * half + j) * TILE, TILE)
        back[:, pl.ds(own, TILE)] = mine[j]
        back[:, pl.ds(far, TILE)] = other[j]


SMEM = pl.BlockSpec(memory_space=pltpu.SMEM)
VMEM = pl.BlockSpec(memory_space=pltpu.VMEM)
FLOPS = 2 * SLOTS * K * TILE * TILE


def sum_copies(parts, copies):
    return pl.pallas_call(
        sum_copies_kernel,
        out_shape=jax.ShapeDtypeStruct((copies,) + parts.shape[1:], jnp.float32),
        in_specs=[VMEM],
        out_specs=VMEM,
        cost_estimate=pl.CostEstimate(
            flops=parts.size, bytes_accessed=4 * (parts.size + copies * parts[0].size), transcendentals=0
        ),
    )(parts)


def per_device(tiles, coords, counts, basis):
    tiles = tiles.reshape(SLOTS, TILE, TILE)
    coords = coords.reshape(2, SLOTS)
    counts = counts.reshape(1)
    core = lax.axis_index("core")
    params = pltpu.CompilerParams(vmem_limit_bytes=16 * 1024 * 1024)
    with jax.named_scope("forward"):
        part = pl.pallas_call(
            forward_kernel,
            out_shape=jax.ShapeDtypeStruct((RT, K, TILE), jnp.float32),
            in_specs=[SMEM, SMEM, VMEM, VMEM],
            out_specs=VMEM,
            compiler_params=params,
            cost_estimate=pl.CostEstimate(flops=FLOPS, bytes_accessed=1900000, transcendentals=0),
        )(coords, counts, tiles, basis)
    with jax.named_scope("image_near_sum"):
        got = lax.all_to_all(part, NEAR, 0, 0, tiled=True)
        near = sum_copies(got, 8)
    with jax.named_scope("image_far_sum"):
        got = lax.all_to_all(near, FAR, 0, 0, tiled=True)
        row_tile = sum_copies(got, RT)
    with jax.named_scope("image_gather"):
        image = lax.all_to_all(row_tile, NEAR, 0, 0, tiled=True)
    with jax.named_scope("image_out"):
        index = lax.axis_index(("x", "yh", "zh", "zl"))
        width = RT * TILE // 128
        own = lax.dynamic_slice(
            image, (index // 8, 0, (index % 8) * width), (1, K, width)
        )[0]
    with jax.named_scope("backward"):
        half = jax.ShapeDtypeStruct((CT // 2, K, TILE), jnp.float32)
        keep, send = pl.pallas_call(
            backward_kernel,
            out_shape=[half, half],
            in_specs=[SMEM, SMEM, SMEM, VMEM, VMEM],
            out_specs=[VMEM, VMEM],
            scratch_shapes=[pltpu.VMEM((CT, K, TILE), jnp.float32)],
            compiler_params=params,
            cost_estimate=pl.CostEstimate(flops=FLOPS, bytes_accessed=1900000, transcendentals=0),
        )(coords, counts, core.reshape(1), tiles, image)
    swap = [(0, 1), (1, 0)]
    with jax.named_scope("back_core_sum"):
        both = keep + lax.ppermute(send, "core", swap)
    with jax.named_scope("back_row_sum"):
        got = lax.all_to_all(both, "yl", 0, 0, tiled=True)
        quarter = sum_copies(got.reshape(4, 4 * K, TILE), 4)
    with jax.named_scope("back_row_gather"):
        mine = lax.all_to_all(quarter.reshape(CT // 2, K, TILE), "yl", 0, 0, tiled=True)
    with jax.named_scope("back_core_gather"):
        other = lax.ppermute(mine, "core", swap)
        back = pl.pallas_call(
            join_kernel,
            out_shape=jax.ShapeDtypeStruct((K, CT * TILE), jnp.float32),
            in_specs=[SMEM, VMEM, VMEM],
            out_specs=VMEM,
            cost_estimate=pl.CostEstimate(flops=0, bytes_accessed=1100000, transcendentals=0),
        )(core.reshape(1), mine, other)
    return own, back


def solution(mesh):
    fine = Mesh(mesh.devices.reshape(SIZES), AXES)
    row = ("yl", "core")
    col = ("x", "yh", "zh", "zl")
    return jax.shard_map(
        per_device,
        mesh=fine,
        in_specs=(
            P(row, col, None, None, None),
            P(row, col, None, None),
            P(row, col),
            P(None, col),
        ),
        out_specs=(P(None, row + col), P(None, col)),
        check_vma=False,
    )
```

```python
import jax
import jax.numpy as jnp
from jax import lax
from jax.experimental import pallas as pl
from jax.experimental.pallas import tpu as pltpu
from jax.sharding import Mesh
from jax.sharding import PartitionSpec as P

K = 32
TILE = 128
RT = 16
CT = 32
SLOTS = 16
GROUP = 4

AXES = ("yl", "core", "x", "yh", "zh", "zl")
SIZES = (4, 2, 4, 2, 4, 4)
NEAR = ("x", "zl")
FAR = ("yh", "zh")


def split(value):
    high = value.astype(jnp.bfloat16)
    low = (value - high.astype(jnp.float32)).astype(jnp.bfloat16)
    return high, low


def dot3(left, right_high, right_low, contract):
    high, low = split(left)
    dims = (((1,), (contract,)), ((), ()))
    both = lax.dot_general(
        jnp.concatenate([high, low], axis=0), right_high, dims, preferred_element_type=jnp.float32
    )
    rest = lax.dot_general(high, right_low, dims, preferred_element_type=jnp.float32)
    rows = left.shape[0]
    return both[:rows] + (both[rows:] + rest)


def forward_kernel(
    counts, coords_in, tiles_in, basis_in, part, high, low, coords_out, coords, tiles, basis, small, wide, slots
):
    copies = [
        pltpu.make_async_copy(coords_in, coords, small.at[0]),
        pltpu.make_async_copy(coords_in, coords_out, small.at[1]),
    ]
    for p in range(4):
        rows = pl.ds(p * (K // 4), K // 4)
        copies.append(pltpu.make_async_copy(basis_in.at[rows], basis.at[rows], wide.at[p]))
    for copy in copies:
        copy.start()
    landed = [pltpu.make_async_copy(tiles_in.at[s], tiles.at[s], slots.at[s]) for s in range(SLOTS)]
    for copy in landed:
        copy.start()
    part[...] = jnp.zeros_like(part)
    for copy in copies:
        copy.wait()
    live = counts[0]
    for first in range(0, SLOTS, GROUP):
        for s in range(first, first + GROUP):
            landed[s].wait()

        @pl.when(first < live)
        def _():
            for s in range(first, first + GROUP):
                high[s], low[s] = split(tiles[s])
            for s in range(first, first + GROUP):
                row = coords[0, s]
                col = pl.multiple_of(coords[1, s] * TILE, TILE)
                product = dot3(basis[:, pl.ds(col, TILE)], high[s], low[s], 1)
                part[row] += jnp.where(s < live, product, 0.0)


def backward_kernel(coords, counts, core, high, low, image, keep, send, acc):
    acc[...] = jnp.zeros_like(acc)
    live = counts[0]
    for first in range(0, SLOTS, GROUP):

        @pl.when(first < live)
        def _():
            for s in range(first, first + GROUP):
                product = dot3(image[coords[0, s]], high[s], low[s], 0)
                acc[coords[1, s]] += jnp.where(s < live, product, 0.0)

    half = CT // 2
    mine = core[0, 0] * half
    keep[...] = acc[pl.ds(mine, half)]
    send[...] = acc[pl.ds(half - mine, half)]


def sum_copies_kernel(parts, copies):
    total = parts[0]
    for p in range(1, parts.shape[0]):
        total = total + parts[p]
    for p in range(copies.shape[0]):
        copies[p] = total


def place_kernel(core_xor, part, *refs):
    back, sems = refs[-2:]
    first = core_xor[0, 0]
    half = CT // 2
    copies = []
    for j in range(half):
        column = pl.multiple_of((first * half + j) * TILE, TILE)
        copies.append(pltpu.make_async_copy(part.at[j], back.at[:, pl.ds(column, TILE)], sems.at[j]))
    for copy in copies:
        copy.start()
    for copy in copies:
        copy.wait()


SMEM = pl.BlockSpec(memory_space=pltpu.SMEM)
VMEM = pl.BlockSpec(memory_space=pltpu.VMEM)
ANY = pl.BlockSpec(memory_space=pl.ANY)
MIB = 1024 * 1024
FLOPS = 2 * SLOTS * K * TILE * TILE


def sum_copies(parts, copies):
    return pl.pallas_call(
        sum_copies_kernel,
        out_shape=pltpu.VMEM((copies,) + parts.shape[1:], jnp.float32),
        in_specs=[VMEM],
        out_specs=VMEM,
        compiler_params=pltpu.CompilerParams(vmem_limit_bytes=2 * MIB),
        cost_estimate=pl.CostEstimate(
            flops=parts.size, bytes_accessed=4 * (parts.size + copies * parts[0].size), transcendentals=0
        ),
    )(parts)


def lane(value):
    return jnp.broadcast_to(value, (8, TILE))


def place(core, part, *back):
    return pl.pallas_call(
        place_kernel,
        out_shape=jax.ShapeDtypeStruct((K, CT * TILE), jnp.float32),
        in_specs=[VMEM, ANY] + [ANY] * len(back),
        out_specs=ANY,
        scratch_shapes=[pltpu.SemaphoreType.DMA((CT // 2,))],
        input_output_aliases={2: 0} if back else {},
        compiler_params=pltpu.CompilerParams(vmem_limit_bytes=2 * MIB),
        cost_estimate=pl.CostEstimate(flops=0, bytes_accessed=600000, transcendentals=0),
    )(core, part, *back)


def per_device(tiles, coords, counts, basis):
    tiles = tiles.reshape(SLOTS, TILE, TILE)
    coords = coords.reshape(2, SLOTS)
    counts = counts.reshape(1)
    index = lax.axis_index(("x", "yh", "zh", "zl"))
    core = lax.axis_index("core")
    width = RT * TILE // 128
    spots = (index // 8, index % 8 * width, lane(core), lane(1 - core))
    params = pltpu.CompilerParams(vmem_limit_bytes=8 * MIB)
    halves = jax.ShapeDtypeStruct((SLOTS, TILE, TILE), jnp.bfloat16)
    with jax.named_scope("forward"):
        part, high, low, places = pl.pallas_call(
            forward_kernel,
            out_shape=[
                jax.ShapeDtypeStruct((RT, K, TILE), jnp.float32),
                halves,
                halves,
                jax.ShapeDtypeStruct((2, SLOTS), jnp.int32),
            ],
            in_specs=[SMEM] + [ANY] * 3,
            out_specs=[VMEM] * 4,
            scratch_shapes=[
                pltpu.SMEM((2, SLOTS), jnp.int32),
                pltpu.VMEM((SLOTS, TILE, TILE), jnp.float32),
                pltpu.VMEM((K, CT * TILE), jnp.float32),
                pltpu.SemaphoreType.DMA((2,)),
                pltpu.SemaphoreType.DMA((4,)),
                pltpu.SemaphoreType.DMA((SLOTS,)),
            ],
            compiler_params=params,
            cost_estimate=pl.CostEstimate(flops=FLOPS, bytes_accessed=1900000, transcendentals=0),
        )(counts, *[pltpu.with_memory_space_constraint(a, pltpu.HBM) for a in (coords, tiles, basis)])
    with jax.named_scope("image_near_sum"):
        got = lax.all_to_all(part, NEAR, 0, 0, tiled=True)
        near = sum_copies(got, 8)
    with jax.named_scope("image_far_sum"):
        got = lax.all_to_all(near, FAR, 0, 0, tiled=True)
        got, counts, *spots = lax.optimization_barrier((got, counts) + spots)
        own_tile, own_column, core_lane, other_lane = spots
        row_tile = sum_copies(got, RT)
    with jax.named_scope("image_gather"):
        image = lax.all_to_all(row_tile, NEAR, 0, 0, tiled=True)
    with jax.named_scope("image_out"):
        own = lax.dynamic_slice(image, (own_tile, 0, own_column), (1, K, width))[0]
    with jax.named_scope("backward"):
        half = jax.ShapeDtypeStruct((CT // 2, K, TILE), jnp.float32)
        keep, send = pl.pallas_call(
            backward_kernel,
            out_shape=[half, half],
            in_specs=[SMEM, SMEM, VMEM, VMEM, VMEM, VMEM],
            out_specs=[VMEM, VMEM],
            scratch_shapes=[pltpu.VMEM((CT, K, TILE), jnp.float32)],
            compiler_params=params,
            cost_estimate=pl.CostEstimate(flops=FLOPS, bytes_accessed=1900000, transcendentals=0),
        )(places, counts, core_lane, high, low, image)
    swap = [(0, 1), (1, 0)]
    with jax.named_scope("back_core_sum"):
        theirs, own = lax.optimization_barrier((lax.ppermute(send, "core", swap), own))
        both = keep + theirs
    with jax.named_scope("back_row_sum"):
        got = lax.all_to_all(both, "yl", 0, 0, tiled=True)
        quarter = sum_copies(got.reshape(4, 4 * K, TILE), 4)
    with jax.named_scope("back_row_gather"):
        mine = lax.all_to_all(quarter.reshape(CT // 2, K, TILE), "yl", 0, 0, tiled=True)
    with jax.named_scope("back_core_gather"):
        other = lax.ppermute(mine, "core", swap)
        back = place(core_lane, mine)
        back = place(other_lane, other, back)
    return own, back


def solution(mesh):
    fine = Mesh(mesh.devices.reshape(SIZES), AXES)
    row = ("yl", "core")
    col = ("x", "yh", "zh", "zl")
    return jax.shard_map(
        per_device,
        mesh=fine,
        in_specs=(
            P(row, col, None, None, None),
            P(row, col, None, None),
            P(row, col),
            P(None, col),
        ),
        out_specs=(P(None, row + col), P(None, col)),
        check_vma=False,
    )
```

```python
import jax
import jax.numpy as jnp
from jax import lax
from jax.experimental import pallas as pl
from jax.experimental.pallas import tpu as pltpu
from jax.sharding import PartitionSpec as P

K = 32
TILE = 128
RT = 16
CT = 32
SLOTS = 16
GROUP = 4


def column(x, yh, z):
    return (x * 2 + yh) * 16 + z


def near_groups():
    order = [(x, z) for x in range(4) for z in NEAR_Z]
    return [[column(x, yh, zh * 4 + z) for x, z in order] for yh in range(2) for zh in range(4)]


def far_groups():
    order = [(yh, zh) for yh in FAR_Y for zh in FAR_Z]
    return [[column(x, yh, zh * 4 + z) for yh, zh in order] for x in range(4) for z in range(4)]


def line_groups():
    return [[y * 2 + core for y in LINE_Y] for core in range(2)]


NEAR_Z = (2, 1, 0, 3)
FAR_Y = (1, 0)
FAR_Z = (2, 3, 1, 0)
LINE_Y = (1, 2, 0, 3)


def exchange(value, axis, groups):
    return lax.all_to_all(value, axis, 0, 0, axis_index_groups=groups, tiled=True)


def split(value):
    high = value.astype(jnp.bfloat16)
    low = (value - high.astype(jnp.float32)).astype(jnp.bfloat16)
    return high, low


def dot3(left, right_high, right_low, contract):
    high, low = split(left)
    dims = (((1,), (contract,)), ((), ()))
    both = lax.dot_general(
        jnp.concatenate([high, low], axis=0), right_high, dims, preferred_element_type=jnp.float32
    )
    rest = lax.dot_general(high, right_low, dims, preferred_element_type=jnp.float32)
    rows = left.shape[0]
    return both[:rows] + (both[rows:] + rest)


def forward_kernel(
    counts, coords_in, tiles_in, basis_in, part, high, low, coords_out, coords, tiles, basis, small, wide, slots
):
    copies = [
        pltpu.make_async_copy(coords_in, coords, small.at[0]),
        pltpu.make_async_copy(coords_in, coords_out, small.at[1]),
    ]
    for p in range(4):
        rows = pl.ds(p * (K // 4), K // 4)
        copies.append(pltpu.make_async_copy(basis_in.at[rows], basis.at[rows], wide.at[p]))
    for copy in copies:
        copy.start()
    landed = [pltpu.make_async_copy(tiles_in.at[s], tiles.at[s], slots.at[s]) for s in range(SLOTS)]
    for copy in landed:
        copy.start()
    part[...] = jnp.zeros_like(part)
    for copy in copies:
        copy.wait()
    live = counts[0]
    for first in range(0, SLOTS, GROUP):
        for s in range(first, first + GROUP):
            landed[s].wait()

        @pl.when(first < live)
        def _():
            for s in range(first, first + GROUP):
                high[s], low[s] = split(tiles[s])
            for s in range(first, first + GROUP):
                row = coords[0, s]
                col = pl.multiple_of(coords[1, s] * TILE, TILE)
                product = dot3(basis[:, pl.ds(col, TILE)], high[s], low[s], 1)
                part[row] += jnp.where(s < live, product, 0.0)


def backward_kernel(coords, counts, core, high, low, image, keep, send, acc):
    acc[...] = jnp.zeros_like(acc)
    live = counts[0]
    for first in range(0, SLOTS, GROUP):

        @pl.when(first < live)
        def _():
            for s in range(first, first + GROUP):
                product = dot3(image[coords[0, s]], high[s], low[s], 0)
                acc[coords[1, s]] += jnp.where(s < live, product, 0.0)

    half = CT // 2
    mine = core[0, 0] * half
    keep[...] = acc[pl.ds(mine, half)]
    send[...] = acc[pl.ds(half - mine, half)]


def sum_copies_kernel(parts, copies):
    total = parts[0]
    for p in range(1, parts.shape[0]):
        total = total + parts[p]
    for p in range(copies.shape[0]):
        copies[p] = total


def place_kernel(core_xor, part, *refs):
    back, sems = refs[-2:]
    first = core_xor[0, 0]
    half = CT // 2
    copies = []
    for j in range(half):
        column = pl.multiple_of((first * half + j) * TILE, TILE)
        copies.append(pltpu.make_async_copy(part.at[j], back.at[:, pl.ds(column, TILE)], sems.at[j]))
    for copy in copies:
        copy.start()
    for copy in copies:
        copy.wait()


SMEM = pl.BlockSpec(memory_space=pltpu.SMEM)
VMEM = pl.BlockSpec(memory_space=pltpu.VMEM)
ANY = pl.BlockSpec(memory_space=pl.ANY)
MIB = 1024 * 1024
FLOPS = 2 * SLOTS * K * TILE * TILE


def sum_copies(parts, copies):
    return pl.pallas_call(
        sum_copies_kernel,
        out_shape=pltpu.VMEM((copies,) + parts.shape[1:], jnp.float32),
        in_specs=[VMEM],
        out_specs=VMEM,
        compiler_params=pltpu.CompilerParams(vmem_limit_bytes=2 * MIB),
        cost_estimate=pl.CostEstimate(
            flops=parts.size, bytes_accessed=4 * (parts.size + copies * parts[0].size), transcendentals=0
        ),
    )(parts)


def lane(value):
    return jnp.broadcast_to(value, (8, TILE))


def place(core, part, *back):
    return pl.pallas_call(
        place_kernel,
        out_shape=jax.ShapeDtypeStruct((K, CT * TILE), jnp.float32),
        in_specs=[VMEM, ANY] + [ANY] * len(back),
        out_specs=ANY,
        scratch_shapes=[pltpu.SemaphoreType.DMA((CT // 2,))],
        input_output_aliases={2: 0} if back else {},
        compiler_params=pltpu.CompilerParams(vmem_limit_bytes=2 * MIB),
        cost_estimate=pl.CostEstimate(flops=0, bytes_accessed=600000, transcendentals=0),
    )(core, part, *back)


def per_device(tiles, coords, counts, basis):
    tiles = tiles.reshape(SLOTS, TILE, TILE)
    coords = coords.reshape(2, SLOTS)
    counts = counts.reshape(1)
    index = lax.axis_index("col")
    core = lax.axis_index("row") % 2
    width = RT * TILE // 128
    spots = (index // 8, index % 8 * width, lane(core), lane(1 - core))
    params = pltpu.CompilerParams(vmem_limit_bytes=8 * MIB)
    halves = jax.ShapeDtypeStruct((SLOTS, TILE, TILE), jnp.bfloat16)
    with jax.named_scope("forward"):
        part, high, low, places = pl.pallas_call(
            forward_kernel,
            out_shape=[
                jax.ShapeDtypeStruct((RT, K, TILE), jnp.float32),
                halves,
                halves,
                jax.ShapeDtypeStruct((2, SLOTS), jnp.int32),
            ],
            in_specs=[SMEM] + [ANY] * 3,
            out_specs=[VMEM] * 4,
            scratch_shapes=[
                pltpu.SMEM((2, SLOTS), jnp.int32),
                pltpu.VMEM((SLOTS, TILE, TILE), jnp.float32),
                pltpu.VMEM((K, CT * TILE), jnp.float32),
                pltpu.SemaphoreType.DMA((2,)),
                pltpu.SemaphoreType.DMA((4,)),
                pltpu.SemaphoreType.DMA((SLOTS,)),
            ],
            compiler_params=params,
            cost_estimate=pl.CostEstimate(flops=FLOPS, bytes_accessed=1900000, transcendentals=0),
        )(counts, *[pltpu.with_memory_space_constraint(a, pltpu.HBM) for a in (coords, tiles, basis)])
    part, counts, *spots = lax.optimization_barrier((part, counts) + spots)
    own_tile, own_column, core_lane, other_lane = spots
    with jax.named_scope("image_near_sum"):
        got = exchange(part, "col", near_groups())
        near = sum_copies(got, 8)
    with jax.named_scope("image_far_sum"):
        got = exchange(near, "col", far_groups())
        row_tile = sum_copies(got, RT)
    with jax.named_scope("image_gather"):
        image = exchange(row_tile, "col", near_groups())
    with jax.named_scope("image_out"):
        own = lax.dynamic_slice(image, (own_tile, 0, own_column), (1, K, width))[0]
    with jax.named_scope("backward"):
        half = jax.ShapeDtypeStruct((CT // 2, K, TILE), jnp.float32)
        keep, send = pl.pallas_call(
            backward_kernel,
            out_shape=[half, half],
            in_specs=[SMEM, SMEM, VMEM, VMEM, VMEM, VMEM],
            out_specs=[VMEM, VMEM],
            scratch_shapes=[pltpu.VMEM((CT, K, TILE), jnp.float32)],
            compiler_params=params,
            cost_estimate=pl.CostEstimate(flops=FLOPS, bytes_accessed=1900000, transcendentals=0),
        )(places, counts, core_lane, high, low, image)
    swap = [(r, r ^ 1) for r in range(8)]
    with jax.named_scope("back_core_sum"):
        theirs, own = lax.optimization_barrier((lax.ppermute(send, "row", swap), own))
        both = keep + theirs
    with jax.named_scope("back_row_sum"):
        got = exchange(both, "row", line_groups())
        quarter = sum_copies(got.reshape(4, 4 * K, TILE), 4)
    with jax.named_scope("back_row_gather"):
        mine = exchange(quarter.reshape(CT // 2, K, TILE), "row", line_groups())
    with jax.named_scope("back_core_gather"):
        other = lax.ppermute(mine, "row", swap)
        back = place(core_lane, mine)
        back = place(other_lane, other, back)
    return own, back


def solution(mesh):
    return jax.shard_map(
        per_device,
        mesh=mesh,
        in_specs=(
            P("row", "col", None, None, None),
            P("row", "col", None, None),
            P("row", "col"),
            P(None, "col"),
        ),
        out_specs=(P(None, ("row", "col")), P(None, "col")),
        check_vma=False,
    )
```

```python
import jax
import jax.numpy as jnp
from jax import lax
from jax.experimental import pallas as pl
from jax.experimental.pallas import tpu as pltpu
from jax.sharding import PartitionSpec as P

K = 32
TILE = 128
RT = 16
CT = 32
SLOTS = 16
BATCH = 4
HALF = CT // 2 * TILE


def device(y, core, x, yh, z):
    return ((y * 2 + core) * 4 + x) * 32 + yh * 16 + z


def near_groups():
    order = [(x, z) for x in NEAR_X for z in NEAR_Z]
    return [
        [device(y, core, x, yh, zh * 4 + z) for x, z in order]
        for y in range(4)
        for core in range(2)
        for yh in range(2)
        for zh in range(4)
    ]


def far_groups():
    order = [(yh, zh) for yh in FAR_Y for zh in FAR_Z]
    return [
        [device(y, core, x, yh, zh * 4 + z) for yh, zh in order]
        for y in range(4)
        for core in range(2)
        for x in range(4)
        for z in range(4)
    ]


def line_groups():
    return [
        [device(y, core, x, yh, z) for y in LINE_Y[yh]]
        for core in range(2)
        for x in range(4)
        for yh in range(2)
        for z in range(16)
    ]


NEAR_X = (2, 1, 3, 0)
NEAR_Z = (2, 1, 0, 3)
FAR_Y = (1, 0)
FAR_Z = (2, 3, 1, 0)
LINE_Y = ((2, 1, 0, 3), (1, 2, 0, 3))


def exchange(value, groups):
    return lax.all_to_all(value, ("row", "col"), 0, 0, axis_index_groups=groups, tiled=True)


def split(value):
    high = value.astype(jnp.bfloat16)
    low = (value - high.astype(jnp.float32)).astype(jnp.bfloat16)
    return high, low


def dot3(left, right_high, right_low, contract):
    high, low = split(left)
    dims = (((1,), (contract,)), ((), ()))
    both = lax.dot_general(
        jnp.concatenate([high, low], axis=0), right_high, dims, preferred_element_type=jnp.float32
    )
    rest = lax.dot_general(high, right_low, dims, preferred_element_type=jnp.float32)
    rows = left.shape[0]
    return both[:rows] + (both[rows:] + rest)


def forward_kernel(
    counts, coords_in, tiles_in, basis_in, part, high, low, coords_out, coords, tiles, basis, small, wide, slots
):
    copies = [
        pltpu.make_async_copy(coords_in, coords, small.at[0]),
        pltpu.make_async_copy(coords_in, coords_out, small.at[1]),
    ]
    copies.append(pltpu.make_async_copy(basis_in, basis, wide.at[0]))
    for t in range(SLOTS // BATCH):
        some = pl.ds(t * BATCH, BATCH)
        copies.append(pltpu.make_async_copy(tiles_in.at[some], tiles.at[some], slots.at[t]))
    for copy in copies:
        copy.start()
    part[...] = jnp.zeros_like(part)
    for copy in copies:
        copy.wait()
    live = counts[0]
    for s in range(SLOTS):
        high[s], low[s] = split(tiles[s])
    for s in range(SLOTS):
        row = coords[0, s]
        col = pl.multiple_of(coords[1, s] * TILE, TILE)
        product = dot3(basis[:, pl.ds(col, TILE)], high[s], low[s], 1)
        part[row] += jnp.where(s < live, product, 0.0)


def backward_kernel(coords, counts, core, high, low, image, keep, send, acc):
    acc[...] = jnp.zeros_like(acc)
    live = counts[0]
    for s in range(SLOTS):
        product = dot3(image[coords[0, s]], high[s], low[s], 0)
        col = pl.multiple_of(coords[1, s] * TILE, TILE)
        acc[:, pl.ds(col, TILE)] += jnp.where(s < live, product, 0.0)
    mine = pl.multiple_of(core[0, 0] * HALF, TILE)
    other = pl.multiple_of(HALF - core[0, 0] * HALF, TILE)
    keep[...] = acc[:, pl.ds(mine, HALF)]
    send[...] = acc[:, pl.ds(other, HALF)]


def sum_copies_kernel(parts, copies):
    total = parts[0]
    for p in range(1, parts.shape[0]):
        total = total + parts[p]
    for p in range(copies.shape[0]):
        copies[p] = total


def place_kernel(half, part, *refs):
    back, sem = refs[-2:]
    column = pl.multiple_of(half[0, 0] * HALF, TILE)
    copy = pltpu.make_async_copy(part, back.at[:, pl.ds(column, HALF)], sem.at[0])
    copy.start()
    copy.wait()


SMEM = pl.BlockSpec(memory_space=pltpu.SMEM)
VMEM = pl.BlockSpec(memory_space=pltpu.VMEM)
ANY = pl.BlockSpec(memory_space=pl.ANY)
MIB = 1024 * 1024
FLOPS = 2 * SLOTS * K * TILE * TILE


def sum_copies(parts, copies):
    return pl.pallas_call(
        sum_copies_kernel,
        out_shape=pltpu.VMEM((copies,) + parts.shape[1:], jnp.float32),
        in_specs=[VMEM],
        out_specs=VMEM,
        compiler_params=pltpu.CompilerParams(vmem_limit_bytes=2 * MIB),
        cost_estimate=pl.CostEstimate(
            flops=parts.size, bytes_accessed=4 * (parts.size + copies * parts[0].size), transcendentals=0
        ),
    )(parts)


def lane(value):
    return jnp.broadcast_to(value, (8, TILE))


def place(half, part, *back):
    return pl.pallas_call(
        place_kernel,
        out_shape=jax.ShapeDtypeStruct((K, CT * TILE), jnp.float32),
        in_specs=[VMEM, ANY] + [ANY] * len(back),
        out_specs=ANY,
        scratch_shapes=[pltpu.SemaphoreType.DMA((1,))],
        input_output_aliases={2: 0} if back else {},
        compiler_params=pltpu.CompilerParams(vmem_limit_bytes=2 * MIB),
        cost_estimate=pl.CostEstimate(flops=0, bytes_accessed=600000, transcendentals=0),
    )(half, part, *back)


def per_device(tiles, coords, counts, basis):
    tiles = tiles.reshape(SLOTS, TILE, TILE)
    coords = coords.reshape(2, SLOTS)
    counts = counts.reshape(1)
    index = lax.axis_index("col")
    core = lax.axis_index("row") % 2
    width = RT * TILE // 128
    spots = (index // 8, index % 8 * width, lane(core), lane(1 - core))
    params = pltpu.CompilerParams(vmem_limit_bytes=8 * MIB)
    halves = jax.ShapeDtypeStruct((SLOTS, TILE, TILE), jnp.bfloat16)
    with jax.named_scope("forward"):
        part, high, low, places = pl.pallas_call(
            forward_kernel,
            out_shape=[
                jax.ShapeDtypeStruct((RT, K, TILE), jnp.float32),
                halves,
                halves,
                jax.ShapeDtypeStruct((2, SLOTS), jnp.int32),
            ],
            in_specs=[SMEM] + [ANY] * 3,
            out_specs=[VMEM] * 4,
            scratch_shapes=[
                pltpu.SMEM((2, SLOTS), jnp.int32),
                pltpu.VMEM((SLOTS, TILE, TILE), jnp.float32),
                pltpu.VMEM((K, CT * TILE), jnp.float32),
                pltpu.SemaphoreType.DMA((2,)),
                pltpu.SemaphoreType.DMA((1,)),
                pltpu.SemaphoreType.DMA((SLOTS // BATCH,)),
            ],
            compiler_params=params,
            cost_estimate=pl.CostEstimate(flops=FLOPS, bytes_accessed=1900000, transcendentals=0),
        )(counts, *[pltpu.with_memory_space_constraint(a, pltpu.HBM) for a in (coords, tiles, basis)])
    part, counts, *spots = lax.optimization_barrier((part, counts) + spots)
    own_tile, own_column, core_lane, other_lane = spots
    with jax.named_scope("image_near_sum"):
        got = exchange(part, near_groups())
        near = sum_copies(got, 8)
    with jax.named_scope("image_far_sum"):
        got = exchange(near, far_groups())
        row_tile = sum_copies(got, RT)
    with jax.named_scope("image_gather"):
        image = exchange(row_tile, near_groups())
    with jax.named_scope("image_out"):
        own = lax.dynamic_slice(image, (own_tile, 0, own_column), (1, K, width))[0]
    with jax.named_scope("backward"):
        half = jax.ShapeDtypeStruct((K, HALF), jnp.float32)
        keep, send = pl.pallas_call(
            backward_kernel,
            out_shape=[half, half],
            in_specs=[SMEM, SMEM, VMEM, VMEM, VMEM, VMEM],
            out_specs=[VMEM, VMEM],
            scratch_shapes=[pltpu.VMEM((K, CT * TILE), jnp.float32)],
            compiler_params=params,
            cost_estimate=pl.CostEstimate(flops=FLOPS, bytes_accessed=1900000, transcendentals=0),
        )(places, counts, core_lane, high, low, image)
    swap = [(r, r ^ 1) for r in range(8)]
    with jax.named_scope("back_core_sum"):
        theirs, own = lax.optimization_barrier((lax.ppermute(send, "row", swap), own))
        both = keep + theirs
    with jax.named_scope("back_row_sum"):
        got = exchange(both, line_groups())
        quarter = sum_copies(got.reshape(4, K // 4, HALF), 4)
    with jax.named_scope("back_row_gather"):
        mine = exchange(quarter.reshape(K, HALF), line_groups())
    with jax.named_scope("back_core_gather"):
        other = lax.ppermute(mine, "row", swap)
        back = place(core_lane, mine)
        back = place(other_lane, other, back)
    return own, back


def solution(mesh):
    return jax.shard_map(
        per_device,
        mesh=mesh,
        in_specs=(
            P("row", "col", None, None, None),
            P("row", "col", None, None),
            P("row", "col"),
            P(None, "col"),
        ),
        out_specs=(P(None, ("row", "col")), P(None, "col")),
        check_vma=False,
    )
```

```python
import jax
import jax.numpy as jnp
from jax import lax
from jax.experimental import pallas as pl
from jax.experimental.pallas import tpu as pltpu
from jax.sharding import PartitionSpec as P

K = 32
TILE = 128
RT = 16
CT = 32
SLOTS = 16
BATCH = 4
HALF = CT // 2 * TILE


def device(y, core, x, yh, z):
    return ((y * 2 + core) * 4 + x) * 32 + yh * 16 + z


def near_groups():
    order = [(x, z) for x in NEAR_X for z in NEAR_Z]
    return [
        [device(y, core, x, yh, zh * 4 + z) for x, z in order]
        for y in range(4)
        for core in range(2)
        for yh in range(2)
        for zh in range(4)
    ]


def far_groups():
    order = [(yh, zh) for yh in FAR_Y for zh in FAR_Z]
    return [
        [device(y, core, x, yh, zh * 4 + z) for yh, zh in order]
        for y in range(4)
        for core in range(2)
        for x in range(4)
        for z in range(4)
    ]


def line_groups():
    return [
        [device(y, core, x, yh, z) for y in LINE_Y[yh]]
        for core in range(2)
        for x in range(4)
        for yh in range(2)
        for z in range(16)
    ]


NEAR_X = (2, 1, 3, 0)
NEAR_Z = (2, 1, 0, 3)
FAR_Y = (1, 0)
FAR_Z = (2, 3, 1, 0)
LINE_Y = ((2, 1, 0, 3), (1, 2, 0, 3))


def exchange(value, groups):
    return lax.all_to_all(value, ("row", "col"), 0, 0, axis_index_groups=groups, tiled=True)


def split(value):
    high = value.astype(jnp.bfloat16)
    low = (value - high.astype(jnp.float32)).astype(jnp.bfloat16)
    return high, low


def dot3(left, right_high, right_low, contract):
    high, low = split(left)
    dims = (((1,), (contract,)), ((), ()))
    both = lax.dot_general(
        jnp.concatenate([high, low], axis=0), right_high, dims, preferred_element_type=jnp.float32
    )
    rest = lax.dot_general(high, right_low, dims, preferred_element_type=jnp.float32)
    rows = left.shape[0]
    return both[:rows] + (both[rows:] + rest)


def forward_kernel(
    counts_in, coords_in, tiles_in, basis_in, part, high, low, places, counts, coords, tiles, basis, small, wide, slots
):
    copies = [
        pltpu.make_async_copy(coords_in, coords, small.at[0]),
        pltpu.make_async_copy(coords_in, places, small.at[1]),
        pltpu.make_async_copy(counts_in, counts, small.at[2]),
    ]
    copies.append(pltpu.make_async_copy(basis_in, basis, wide.at[0]))
    for t in range(SLOTS // BATCH):
        some = pl.ds(t * BATCH, BATCH)
        copies.append(pltpu.make_async_copy(tiles_in.at[some], tiles.at[some], slots.at[t]))
    for copy in copies:
        copy.start()
    part[...] = jnp.zeros_like(part)
    for copy in copies:
        copy.wait()
    live = counts[0]
    slot = lax.broadcasted_iota(jnp.int32, places.shape, 1)
    places[...] = jnp.where(slot < live, places[...], -1)
    for s in range(SLOTS):
        high[s], low[s] = split(tiles[s])
    for s in range(SLOTS):
        row = coords[0, s]
        col = pl.multiple_of(coords[1, s] * TILE, TILE)
        product = dot3(basis[:, pl.ds(col, TILE)], high[s], low[s], 1)
        part[row] += jnp.where(s < live, product, 0.0)


def backward_kernel(places, core, high, low, image, keep, send, acc):
    acc[...] = jnp.zeros_like(acc)
    for s in range(SLOTS):
        row = places[0, s]
        product = dot3(image[jnp.maximum(row, 0)], high[s], low[s], 0)
        col = pl.multiple_of(jnp.maximum(places[1, s], 0) * TILE, TILE)
        acc[:, pl.ds(col, TILE)] += jnp.where(row >= 0, product, 0.0)
    mine = pl.multiple_of(core[0, 0] * HALF, TILE)
    other = pl.multiple_of(HALF - core[0, 0] * HALF, TILE)
    keep[...] = acc[:, pl.ds(mine, HALF)]
    send[...] = acc[:, pl.ds(other, HALF)]


def sum_copies_kernel(parts, copies):
    total = parts[0]
    for p in range(1, parts.shape[0]):
        total = total + parts[p]
    for p in range(copies.shape[0]):
        copies[p] = total


def place_kernel(half, part, *refs):
    back, sem = refs[-2:]
    column = pl.multiple_of(half[0, 0] * HALF, TILE)
    copy = pltpu.make_async_copy(part, back.at[:, pl.ds(column, HALF)], sem.at[0])
    copy.start()
    copy.wait()


SMEM = pl.BlockSpec(memory_space=pltpu.SMEM)
VMEM = pl.BlockSpec(memory_space=pltpu.VMEM)
ANY = pl.BlockSpec(memory_space=pl.ANY)
MIB = 1024 * 1024
FLOPS = 2 * SLOTS * K * TILE * TILE


def sum_copies(parts, copies):
    return pl.pallas_call(
        sum_copies_kernel,
        out_shape=pltpu.VMEM((copies,) + parts.shape[1:], jnp.float32),
        in_specs=[VMEM],
        out_specs=VMEM,
        compiler_params=pltpu.CompilerParams(vmem_limit_bytes=2 * MIB),
        cost_estimate=pl.CostEstimate(
            flops=parts.size, bytes_accessed=4 * (parts.size + copies * parts[0].size), transcendentals=0
        ),
    )(parts)


def lane(value):
    return jnp.broadcast_to(value, (8, TILE))


def place(half, part, *back):
    return pl.pallas_call(
        place_kernel,
        out_shape=jax.ShapeDtypeStruct((K, CT * TILE), jnp.float32),
        in_specs=[VMEM, ANY] + [ANY] * len(back),
        out_specs=ANY,
        scratch_shapes=[pltpu.SemaphoreType.DMA((1,))],
        input_output_aliases={2: 0} if back else {},
        compiler_params=pltpu.CompilerParams(vmem_limit_bytes=2 * MIB),
        cost_estimate=pl.CostEstimate(flops=0, bytes_accessed=600000, transcendentals=0),
    )(half, part, *back)


def per_device(tiles, coords, counts, basis):
    tiles = tiles.reshape(SLOTS, TILE, TILE)
    coords = coords.reshape(2, SLOTS)
    counts = counts.reshape(1)
    index = lax.axis_index("col")
    core = lax.axis_index("row") % 2
    width = RT * TILE // 128
    spots = (index // 8, index % 8 * width, lane(core), lane(1 - core))
    params = pltpu.CompilerParams(vmem_limit_bytes=8 * MIB)
    halves = jax.ShapeDtypeStruct((SLOTS, TILE, TILE), jnp.bfloat16)
    with jax.named_scope("forward"):
        part, high, low, places = pl.pallas_call(
            forward_kernel,
            out_shape=[
                jax.ShapeDtypeStruct((RT, K, TILE), jnp.float32),
                halves,
                halves,
                jax.ShapeDtypeStruct((2, SLOTS), jnp.int32),
            ],
            in_specs=[ANY] * 4,
            out_specs=[VMEM] * 4,
            scratch_shapes=[
                pltpu.SMEM((1,), jnp.int32),
                pltpu.SMEM((2, SLOTS), jnp.int32),
                pltpu.VMEM((SLOTS, TILE, TILE), jnp.float32),
                pltpu.VMEM((K, CT * TILE), jnp.float32),
                pltpu.SemaphoreType.DMA((3,)),
                pltpu.SemaphoreType.DMA((1,)),
                pltpu.SemaphoreType.DMA((SLOTS // BATCH,)),
            ],
            compiler_params=params,
            cost_estimate=pl.CostEstimate(flops=FLOPS, bytes_accessed=1900000, transcendentals=0),
        )(counts, *[pltpu.with_memory_space_constraint(a, pltpu.HBM) for a in (coords, tiles, basis)])
    part, *spots = lax.optimization_barrier((part,) + spots)
    own_tile, own_column, core_lane, other_lane = spots
    with jax.named_scope("image_near_sum"):
        got = exchange(part, near_groups())
        near = sum_copies(got, 8)
    with jax.named_scope("image_far_sum"):
        got = exchange(near, far_groups())
        row_tile = sum_copies(got, RT)
    with jax.named_scope("image_gather"):
        image = exchange(row_tile, near_groups())
    with jax.named_scope("image_out"):
        own = lax.dynamic_slice(image, (own_tile, 0, own_column), (1, K, width))[0]
    with jax.named_scope("backward"):
        half = jax.ShapeDtypeStruct((K, HALF), jnp.float32)
        keep, send = pl.pallas_call(
            backward_kernel,
            out_shape=[half, half],
            in_specs=[VMEM, VMEM, VMEM, VMEM, VMEM],
            out_specs=[VMEM, VMEM],
            scratch_shapes=[pltpu.VMEM((K, CT * TILE), jnp.float32)],
            compiler_params=params,
            cost_estimate=pl.CostEstimate(flops=FLOPS, bytes_accessed=1900000, transcendentals=0),
        )(places, core_lane, high, low, image)
    swap = [(r, r ^ 1) for r in range(8)]
    with jax.named_scope("back_core_sum"):
        theirs, own = lax.optimization_barrier((lax.ppermute(send, "row", swap), own))
        both = keep + theirs
    with jax.named_scope("back_row_sum"):
        got = exchange(both, line_groups())
        quarter = sum_copies(got.reshape(4, K // 4, HALF), 4)
    with jax.named_scope("back_row_gather"):
        mine = exchange(quarter.reshape(K, HALF), line_groups())
    with jax.named_scope("back_core_gather"):
        other = lax.ppermute(mine, "row", swap)
        back = place(core_lane, mine)
        back = place(other_lane, other, back)
    return own, back


def solution(mesh):
    return jax.shard_map(
        per_device,
        mesh=mesh,
        in_specs=(
            P("row", "col", None, None, None),
            P("row", "col", None, None),
            P("row", "col"),
            P(None, "col"),
        ),
        out_specs=(P(None, ("row", "col")), P(None, "col")),
        check_vma=False,
    )
```

```python
import jax
import jax.numpy as jnp
from jax import lax
from jax.experimental import pallas as pl
from jax.experimental.pallas import tpu as pltpu
from jax.sharding import PartitionSpec as P

K = 32
TILE = 128
RT = 16
CT = 32
SLOTS = 16
BATCH = 8
HALF = CT // 2 * TILE


def device(y, core, x, yh, z):
    return ((y * 2 + core) * 4 + x) * 32 + yh * 16 + z


def near_groups():
    order = [NEAR_FIRST] + [(x, z) for z in range(4) for x in range(4) if (x, z) != NEAR_FIRST]
    return [
        [device(y, core, x, yh, zh * 4 + z) for x, z in order]
        for y in range(4)
        for core in range(2)
        for yh in range(2)
        for zh in range(4)
    ]


def far_groups():
    order = [FAR_FIRST] + [(yh, zh) for zh in range(4) for yh in range(2) if (yh, zh) != FAR_FIRST]
    return [
        [device(y, core, x, yh, zh * 4 + z) for yh, zh in order]
        for y in range(4)
        for core in range(2)
        for x in range(4)
        for z in range(4)
    ]


def line_groups():
    return [
        [device(y, core, x, yh, z) for y in LINE_Y[yh]]
        for core in range(2)
        for x in range(4)
        for yh in range(2)
        for z in range(16)
    ]


NEAR_FIRST = (2, 2)
FAR_FIRST = (1, 2)
LINE_Y = ((2, 1, 0, 3), (1, 2, 0, 3))


def exchange(value, groups):
    return lax.all_to_all(value, ("row", "col"), 0, 0, axis_index_groups=groups, tiled=True)


def split(value):
    high = value.astype(jnp.bfloat16)
    low = (value - high.astype(jnp.float32)).astype(jnp.bfloat16)
    return high, low


def dot3(left, right_high, right_low, contract):
    high, low = split(left)
    dims = (((1,), (contract,)), ((), ()))
    both = lax.dot_general(
        jnp.concatenate([high, low], axis=0), right_high, dims, preferred_element_type=jnp.float32
    )
    rest = lax.dot_general(high, right_low, dims, preferred_element_type=jnp.float32)
    rows = left.shape[0]
    return both[:rows] + (both[rows:] + rest)


def forward_kernel(
    counts_in, coords_in, tiles_in, basis_in, part, high, low, places, counts, coords, tiles, basis, small, wide, slots
):
    copies = [
        pltpu.make_async_copy(coords_in, coords, small.at[0]),
        pltpu.make_async_copy(coords_in, places, small.at[1]),
        pltpu.make_async_copy(counts_in, counts, small.at[2]),
    ]
    copies.append(pltpu.make_async_copy(basis_in, basis, wide.at[0]))
    for t in range(SLOTS // BATCH):
        some = pl.ds(t * BATCH, BATCH)
        copies.append(pltpu.make_async_copy(tiles_in.at[some], tiles.at[some], slots.at[t]))
    for copy in copies:
        copy.start()
    part[...] = jnp.zeros_like(part)
    for copy in copies:
        copy.wait()
    live = counts[0]
    slot = lax.broadcasted_iota(jnp.int32, places.shape, 1)
    places[...] = jnp.where(slot < live, places[...], -1)
    for s in range(SLOTS):
        high[s], low[s] = split(tiles[s])
    for s in range(SLOTS):
        row = coords[0, s]
        col = pl.multiple_of(coords[1, s] * TILE, TILE)
        product = dot3(basis[:, pl.ds(col, TILE)], high[s], low[s], 1)
        part[row] += jnp.where(s < live, product, 0.0)


def backward_kernel(places, core, high, low, image, keep, send, acc):
    acc[...] = jnp.zeros_like(acc)
    for s in range(SLOTS):
        row = places[0, s]
        product = dot3(image[jnp.maximum(row, 0)], high[s], low[s], 0)
        col = pl.multiple_of(jnp.maximum(places[1, s], 0) * TILE, TILE)
        acc[:, pl.ds(col, TILE)] += jnp.where(row >= 0, product, 0.0)
    mine = pl.multiple_of(core[0, 0] * HALF, TILE)
    other = pl.multiple_of(HALF - core[0, 0] * HALF, TILE)
    keep[...] = acc[:, pl.ds(mine, HALF)]
    send[...] = acc[:, pl.ds(other, HALF)]


def sum_copies_kernel(parts, copies):
    total = parts[0]
    for p in range(1, parts.shape[0]):
        total = total + parts[p]
    for p in range(copies.shape[0]):
        copies[p] = total


def place_kernel(half, part, *refs):
    back, sem = refs[-2:]
    column = pl.multiple_of(half[0, 0] * HALF, TILE)
    copy = pltpu.make_async_copy(part, back.at[:, pl.ds(column, HALF)], sem.at[0])
    copy.start()
    copy.wait()


SMEM = pl.BlockSpec(memory_space=pltpu.SMEM)
VMEM = pl.BlockSpec(memory_space=pltpu.VMEM)
ANY = pl.BlockSpec(memory_space=pl.ANY)
MIB = 1024 * 1024
FLOPS = 2 * SLOTS * K * TILE * TILE


def sum_copies(parts, copies):
    return pl.pallas_call(
        sum_copies_kernel,
        out_shape=pltpu.VMEM((copies,) + parts.shape[1:], jnp.float32),
        in_specs=[VMEM],
        out_specs=VMEM,
        compiler_params=pltpu.CompilerParams(vmem_limit_bytes=2 * MIB),
        cost_estimate=pl.CostEstimate(
            flops=parts.size, bytes_accessed=4 * (parts.size + copies * parts[0].size), transcendentals=0
        ),
    )(parts)


def lane(value):
    return jnp.broadcast_to(value, (8, TILE))


def place(half, part, *back):
    return pl.pallas_call(
        place_kernel,
        out_shape=jax.ShapeDtypeStruct((K, CT * TILE), jnp.float32),
        in_specs=[VMEM, ANY] + [ANY] * len(back),
        out_specs=ANY,
        scratch_shapes=[pltpu.SemaphoreType.DMA((1,))],
        input_output_aliases={2: 0} if back else {},
        compiler_params=pltpu.CompilerParams(vmem_limit_bytes=2 * MIB),
        cost_estimate=pl.CostEstimate(flops=0, bytes_accessed=600000, transcendentals=0),
    )(half, part, *back)


def per_device(tiles, coords, counts, basis):
    tiles = tiles.reshape(SLOTS, TILE, TILE)
    coords = coords.reshape(2, SLOTS)
    counts = counts.reshape(1)
    index = lax.axis_index("col")
    core = lax.axis_index("row") % 2
    width = RT * TILE // 128
    spots = (index // 8, index % 8 * width, lane(core), lane(1 - core))
    params = pltpu.CompilerParams(vmem_limit_bytes=8 * MIB)
    halves = jax.ShapeDtypeStruct((SLOTS, TILE, TILE), jnp.bfloat16)
    with jax.named_scope("forward"):
        part, high, low, places = pl.pallas_call(
            forward_kernel,
            out_shape=[
                jax.ShapeDtypeStruct((RT, K, TILE), jnp.float32),
                halves,
                halves,
                jax.ShapeDtypeStruct((2, SLOTS), jnp.int32),
            ],
            in_specs=[ANY] * 4,
            out_specs=[VMEM] * 4,
            scratch_shapes=[
                pltpu.SMEM((1,), jnp.int32),
                pltpu.SMEM((2, SLOTS), jnp.int32),
                pltpu.VMEM((SLOTS, TILE, TILE), jnp.float32),
                pltpu.VMEM((K, CT * TILE), jnp.float32),
                pltpu.SemaphoreType.DMA((3,)),
                pltpu.SemaphoreType.DMA((1,)),
                pltpu.SemaphoreType.DMA((SLOTS // BATCH,)),
            ],
            compiler_params=params,
            cost_estimate=pl.CostEstimate(flops=FLOPS, bytes_accessed=1900000, transcendentals=0),
        )(counts, *[pltpu.with_memory_space_constraint(a, pltpu.HBM) for a in (coords, tiles, basis)])
    part, *spots = lax.optimization_barrier((part,) + spots)
    own_tile, own_column, core_lane, other_lane = spots
    with jax.named_scope("image_near_sum"):
        got = exchange(part, near_groups())
        near = sum_copies(got, 8)
    with jax.named_scope("image_far_sum"):
        got = exchange(near, far_groups())
        row_tile = sum_copies(got, RT)
    with jax.named_scope("image_gather"):
        image = exchange(row_tile, near_groups())
    with jax.named_scope("image_out"):
        own = lax.dynamic_slice(image, (own_tile, 0, own_column), (1, K, width))[0]
    with jax.named_scope("backward"):
        half = jax.ShapeDtypeStruct((K, HALF), jnp.float32)
        keep, send = pl.pallas_call(
            backward_kernel,
            out_shape=[half, half],
            in_specs=[VMEM, VMEM, VMEM, VMEM, VMEM],
            out_specs=[VMEM, VMEM],
            scratch_shapes=[pltpu.VMEM((K, CT * TILE), jnp.float32)],
            compiler_params=params,
            cost_estimate=pl.CostEstimate(flops=FLOPS, bytes_accessed=1900000, transcendentals=0),
        )(places, core_lane, high, low, image)
    swap = [(r, r ^ 1) for r in range(8)]
    with jax.named_scope("back_core_sum"):
        theirs, own = lax.optimization_barrier((lax.ppermute(send, "row", swap), own))
        both = keep + theirs
    with jax.named_scope("back_row_sum"):
        got = exchange(both, line_groups())
        quarter = sum_copies(got.reshape(4, K // 4, HALF), 4)
    with jax.named_scope("back_row_gather"):
        mine = exchange(quarter.reshape(K, HALF), line_groups())
    with jax.named_scope("back_core_gather"):
        other = lax.ppermute(mine, "row", swap)
        back = place(core_lane, mine)
        back = place(other_lane, other, back)
    return own, back


def solution(mesh):
    return jax.shard_map(
        per_device,
        mesh=mesh,
        in_specs=(
            P("row", "col", None, None, None),
            P("row", "col", None, None),
            P("row", "col"),
            P(None, "col"),
        ),
        out_specs=(P(None, ("row", "col")), P(None, "col")),
        check_vma=False,
    )
```

```python
import jax
import jax.numpy as jnp
from jax import lax
from jax.experimental import pallas as pl
from jax.experimental.pallas import tpu as pltpu
from jax.sharding import PartitionSpec as P

K = 32
TILE = 128
RT = 16
CT = 32
SLOTS = 16
BATCH = 4
HALF = CT // 2 * TILE


def device(y, core, x, yh, z):
    return ((y * 2 + core) * 4 + x) * 32 + yh * 16 + z


def near_groups():
    order = [(x, z) for x in NEAR_X for z in NEAR_Z]
    return [
        [device(y, core, x, yh, zh * 4 + z) for x, z in order]
        for y in range(4)
        for core in range(2)
        for yh in range(2)
        for zh in range(4)
    ]


def far_groups():
    order = [(yh, zh) for yh in FAR_Y for zh in FAR_Z]
    return [
        [device(y, core, x, yh, zh * 4 + z) for yh, zh in order]
        for y in range(4)
        for core in range(2)
        for x in range(4)
        for z in range(4)
    ]


def line_groups():
    return [
        [device(y, core, x, yh, z) for y in LINE_Y[yh]]
        for core in range(2)
        for x in range(4)
        for yh in range(2)
        for z in range(16)
    ]


NEAR_X = (2, 1, 3, 0)
NEAR_Z = (2, 1, 0, 3)
FAR_Y = (1, 0)
FAR_Z = (2, 3, 1, 0)
LINE_Y = ((2, 1, 0, 3), (1, 2, 0, 3))


def exchange(value, groups):
    return lax.all_to_all(value, ("row", "col"), 0, 0, axis_index_groups=groups, tiled=True)


def split(value):
    high = value.astype(jnp.bfloat16)
    low = (value - high.astype(jnp.float32)).astype(jnp.bfloat16)
    return high, low


def dot3(left, right_high, right_low, contract):
    high, low = split(left)
    dims = (((1,), (contract,)), ((), ()))
    both = lax.dot_general(
        jnp.concatenate([high, low], axis=0), right_high, dims, preferred_element_type=jnp.float32
    )
    rest = lax.dot_general(high, right_low, dims, preferred_element_type=jnp.float32)
    rows = left.shape[0]
    return both[:rows] + (both[rows:] + rest)


def forward_kernel(
    counts_in, coords_in, tiles_in, basis_in, part, high, low, places, counts, coords, tiles, basis, small, wide, slots
):
    copies = [
        pltpu.make_async_copy(coords_in, coords, small.at[0]),
        pltpu.make_async_copy(coords_in, places, small.at[1]),
        pltpu.make_async_copy(counts_in, counts, small.at[2]),
    ]
    for t in range(SLOTS // BATCH):
        some = pl.ds(t * BATCH, BATCH)
        copies.append(pltpu.make_async_copy(tiles_in.at[some], tiles.at[some], slots.at[t]))
    copies.append(pltpu.make_async_copy(basis_in, basis, wide.at[0]))
    for copy in copies:
        copy.start()
    part[...] = jnp.zeros_like(part)
    for copy in copies[:-1]:
        copy.wait()
    live = counts[0]
    slot = lax.broadcasted_iota(jnp.int32, places.shape, 1)
    places[...] = jnp.where(slot < live, places[...], -1)
    for s in range(SLOTS):
        high[s], low[s] = split(tiles[s])
    copies[-1].wait()
    for s in range(SLOTS):
        row = coords[0, s]
        col = pl.multiple_of(coords[1, s] * TILE, TILE)
        product = dot3(basis[:, pl.ds(col, TILE)], high[s], low[s], 1)
        part[row] += jnp.where(s < live, product, 0.0)


def backward_kernel(places, core, high, low, image, keep, send, acc):
    acc[...] = jnp.zeros_like(acc)
    for s in range(SLOTS):
        row = places[0, s]
        product = dot3(image[jnp.maximum(row, 0)], high[s], low[s], 0)
        col = pl.multiple_of(jnp.maximum(places[1, s], 0) * TILE, TILE)
        acc[:, pl.ds(col, TILE)] += jnp.where(row >= 0, product, 0.0)
    mine = pl.multiple_of(core[0, 0] * HALF, TILE)
    other = pl.multiple_of(HALF - core[0, 0] * HALF, TILE)
    keep[...] = acc[:, pl.ds(mine, HALF)]
    send[...] = acc[:, pl.ds(other, HALF)]


def sum_copies_kernel(parts, copies):
    total = parts[0]
    for p in range(1, parts.shape[0]):
        total = total + parts[p]
    for p in range(copies.shape[0]):
        copies[p] = total


def place_kernel(half, part, *refs):
    back, sem = refs[-2:]
    column = pl.multiple_of(half[0, 0] * HALF, TILE)
    copy = pltpu.make_async_copy(part, back.at[:, pl.ds(column, HALF)], sem.at[0])
    copy.start()
    copy.wait()


SMEM = pl.BlockSpec(memory_space=pltpu.SMEM)
VMEM = pl.BlockSpec(memory_space=pltpu.VMEM)
ANY = pl.BlockSpec(memory_space=pl.ANY)
MIB = 1024 * 1024
FLOPS = 2 * SLOTS * K * TILE * TILE


def sum_copies(parts, copies):
    return pl.pallas_call(
        sum_copies_kernel,
        out_shape=pltpu.VMEM((copies,) + parts.shape[1:], jnp.float32),
        in_specs=[VMEM],
        out_specs=VMEM,
        compiler_params=pltpu.CompilerParams(vmem_limit_bytes=2 * MIB),
        cost_estimate=pl.CostEstimate(
            flops=parts.size, bytes_accessed=4 * (parts.size + copies * parts[0].size), transcendentals=0
        ),
    )(parts)


def lane(value):
    return jnp.broadcast_to(value, (8, TILE))


def place(half, part, *back):
    return pl.pallas_call(
        place_kernel,
        out_shape=jax.ShapeDtypeStruct((K, CT * TILE), jnp.float32),
        in_specs=[VMEM, ANY] + [ANY] * len(back),
        out_specs=ANY,
        scratch_shapes=[pltpu.SemaphoreType.DMA((1,))],
        input_output_aliases={2: 0} if back else {},
        compiler_params=pltpu.CompilerParams(vmem_limit_bytes=2 * MIB),
        cost_estimate=pl.CostEstimate(flops=0, bytes_accessed=600000, transcendentals=0),
    )(half, part, *back)


def per_device(tiles, coords, counts, basis):
    tiles = tiles.reshape(SLOTS, TILE, TILE)
    coords = coords.reshape(2, SLOTS)
    counts = counts.reshape(1)
    index = lax.axis_index("col")
    core = lax.axis_index("row") % 2
    width = RT * TILE // 128
    spots = (index // 8, index % 8 * width, lane(core), lane(1 - core))
    params = pltpu.CompilerParams(vmem_limit_bytes=8 * MIB)
    halves = jax.ShapeDtypeStruct((SLOTS, TILE, TILE), jnp.bfloat16)
    with jax.named_scope("forward"):
        part, high, low, places = pl.pallas_call(
            forward_kernel,
            out_shape=[
                jax.ShapeDtypeStruct((RT, K, TILE), jnp.float32),
                halves,
                halves,
                jax.ShapeDtypeStruct((2, SLOTS), jnp.int32),
            ],
            in_specs=[ANY] * 4,
            out_specs=[VMEM] * 4,
            scratch_shapes=[
                pltpu.SMEM((1,), jnp.int32),
                pltpu.SMEM((2, SLOTS), jnp.int32),
                pltpu.VMEM((SLOTS, TILE, TILE), jnp.float32),
                pltpu.VMEM((K, CT * TILE), jnp.float32),
                pltpu.SemaphoreType.DMA((3,)),
                pltpu.SemaphoreType.DMA((1,)),
                pltpu.SemaphoreType.DMA((SLOTS // BATCH,)),
            ],
            compiler_params=params,
            cost_estimate=pl.CostEstimate(flops=FLOPS, bytes_accessed=1900000, transcendentals=0),
        )(counts, *[pltpu.with_memory_space_constraint(a, pltpu.HBM) for a in (coords, tiles, basis)])
    part, *spots = lax.optimization_barrier((part,) + spots)
    own_tile, own_column, core_lane, other_lane = spots
    with jax.named_scope("image_near_sum"):
        got = exchange(part, near_groups())
        near = sum_copies(got, 8)
    with jax.named_scope("image_far_sum"):
        got = exchange(near, far_groups())
        row_tile = sum_copies(got, RT)
    with jax.named_scope("image_gather"):
        image = exchange(row_tile, near_groups())
    with jax.named_scope("image_out"):
        own = lax.dynamic_slice(image, (own_tile, 0, own_column), (1, K, width))[0]
    with jax.named_scope("backward"):
        half = jax.ShapeDtypeStruct((K, HALF), jnp.float32)
        keep, send = pl.pallas_call(
            backward_kernel,
            out_shape=[half, half],
            in_specs=[VMEM, VMEM, VMEM, VMEM, VMEM],
            out_specs=[VMEM, VMEM],
            scratch_shapes=[pltpu.VMEM((K, CT * TILE), jnp.float32)],
            compiler_params=params,
            cost_estimate=pl.CostEstimate(flops=FLOPS, bytes_accessed=1900000, transcendentals=0),
        )(places, core_lane, high, low, image)
    swap = [(r, r ^ 1) for r in range(8)]
    with jax.named_scope("back_core_sum"):
        theirs, own = lax.optimization_barrier((lax.ppermute(send, "row", swap), own))
        both = keep + theirs
    with jax.named_scope("back_row_sum"):
        got = exchange(both, line_groups())
        quarter = sum_copies(got.reshape(4, K // 4, HALF), 4)
    with jax.named_scope("back_row_gather"):
        mine = exchange(quarter.reshape(K, HALF), line_groups())
    with jax.named_scope("back_core_gather"):
        other = lax.ppermute(mine, "row", swap)
        back = place(core_lane, mine)
        back = place(other_lane, other, back)
    return own, back


def solution(mesh):
    return jax.shard_map(
        per_device,
        mesh=mesh,
        in_specs=(
            P("row", "col", None, None, None),
            P("row", "col", None, None),
            P("row", "col"),
            P(None, "col"),
        ),
        out_specs=(P(None, ("row", "col")), P(None, "col")),
        check_vma=False,
    )
```
